32 devices in a mesh: groups: 2 (over x), feat: 16 (over z, y, core).
Axes of the slice: x: 2, y: 2, z: 4, core: 2. Of those that a mesh axis runs over, the one named last changes fastest.
Arguments:
- features: bfloat16 [1024, 8192], P('feat', 'groups'), parts along dimension 1, may hold values from -6 to 6
- weight_self: bfloat16 [1024, 256], replicated, may hold values from -0.1875 to 0.1875
- weight_neighbor: bfloat16 [1024, 256], replicated, may hold values from -0.1875 to 0.1875
- cotangent: bfloat16 [4096, 256], P(('groups', 'feat')), parts along dimension 0, may hold values from -0.25 to 0.25
- source_tiles: int32 [32, 16], P('groups'), parts along dimension 0, may hold values from 0 to 31
- neighbor_slots: int32 [4096, 10], P('groups'), parts along dimension 0, may hold values from 0 to 2047
- neighbor_counts: int32 [4096], P('groups'), parts along dimension 0, may hold values from 1 to 10
Outputs:
- activated: bfloat16 [4096, 256], P(('groups', 'feat')), parts along dimension 0
- grad_self: float32 [2048, 256], P(('groups', 'feat')), parts along dimension 0
- grad_neighbor: float32 [2048, 256], P(('groups', 'feat')), parts along dimension 0
The draws below stay inside these ranges and needn't reach their ends.
There are 2 independent parts, one for each index of `groups`. The reference program is written for one: setup_inputs(seed, part) draws one part's arguments, and reference() takes and returns one part's arrays. A program takes and returns all parts, laid end to end along the dimension named above; an argument that names none is the same for every part. Nothing has to cross between parts.
All inputs are finite; a program needn't handle non-finite values.
Results may differ from the reference program's by a relative error of at most 0.0045.
Values may be sent and summed in bfloat16 or wider, within the bound.
A program may use at most 128 MiB of HBM per device.

```python
import jax
import jax.numpy as jnp
from jax import lax

F = 1024
H = 256
K = 10
S = 16
DST = 2048
SRC = 4096


def draw_source_tiles(key, part):
    key = jax.random.fold_in(key, 11)
    tile_ids = jax.random.randint(key, (DST // 128, S), 0, 2 * DST // 128, dtype=jnp.int32)
    tile_ids = tile_ids.at[0, 0].set(0)
    tile_ids = tile_ids.at[DST // 128 - 1, S - 1].set(2 * DST // 128 - 1)
    return tile_ids


def draw_neighbor_slots(key, part):
    key = jax.random.fold_in(key, 23)
    slot_ids = jax.random.randint(key, (DST, K), 0, S * 128, dtype=jnp.int32)
    slot_ids = slot_ids.at[0, 0].set(S * 128 - 1)
    slot_ids = slot_ids.at[1, 0].set(0)
    return slot_ids


def draw_neighbor_counts(key, part):
    key = jax.random.fold_in(key, 37)
    counted = jax.random.randint(key, (DST,), 1, K + 1, dtype=jnp.int32)
    counted = counted.at[0].set(K)
    counted = counted.at[1].set(1)
    return counted


def shard_levels(stream_key, shape, pieces, least, top_value):
    level, own = 1.0, jax.random.fold_in(stream_key, 6)
    for position, parts in pieces:
        heights = jnp.exp(jax.random.uniform(jax.random.fold_in(own, position), (parts,), jnp.float32, least / len(pieces), top_value / len(pieces)))
        level = level * jnp.repeat(heights, shape[position] // parts).reshape([-1 if axis == position else 1 for axis in range(len(shape))])
    return level


def scatter_about(rng, extent, width, most, cuts=(), kind=jnp.bfloat16):
    entries = jax.random.normal(rng, extent, jnp.float32) * width
    if len(cuts) > 0:
        entries = shard_levels(rng, extent, cuts, -0.22, 0.18) * entries
    return jnp.clip(entries, min=-most, max=most).astype(kind)


def setup_inputs(seed: int = 0, part: int = 0) -> dict:
    key_list = jax.random.split(jax.random.key(seed), 8)
    part_splits = jax.random.split(jax.random.fold_in(key_list[7], part), 8)
    features = scatter_about(part_splits[0], (F, SRC), 1.0, 6.0, ((0, 16),))
    weight_self = scatter_about(key_list[1], (F, H), F ** -0.5, 0.1875)
    weight_neighbor = scatter_about(key_list[2], (F, H), F ** -0.5, 0.1875)
    cotangent = scatter_about(part_splits[3], (DST, H), (DST // 4) ** -0.5, 0.25, ((0, 16),))
    source_tiles = draw_source_tiles(jax.random.fold_in(jax.random.fold_in(key_list[7], part), 71), part)
    neighbor_slots = draw_neighbor_slots(jax.random.fold_in(jax.random.fold_in(key_list[7], part), 71), part)
    neighbor_counts = draw_neighbor_counts(jax.random.fold_in(jax.random.fold_in(key_list[7], part), 71), part)
    return dict(features=features, weight_self=weight_self, weight_neighbor=weight_neighbor, cotangent=cotangent, source_tiles=source_tiles, neighbor_slots=neighbor_slots, neighbor_counts=neighbor_counts)


def aggregate(features, source_tiles, neighbor_slots, neighbor_counts):
    dst_nodes = neighbor_counts.shape[0]
    fanout = neighbor_slots.shape[1]
    tile_rows = (jnp.arange(dst_nodes, dtype=jnp.int32) // 128).astype(jnp.int32)
    picked = source_tiles[tile_rows[:, None], neighbor_slots // 128]
    sources = (picked * 128 + neighbor_slots % 128).astype(jnp.int32)
    used = jnp.arange(fanout, dtype=jnp.int32)[None, :] < neighbor_counts[:, None]
    scales = jnp.where(used, 1.0, 0.0).astype(jnp.float32) / neighbor_counts[:, None].astype(jnp.float32)

    def add_slot(column, summed):
        index_col = lax.dynamic_index_in_dim(sources, column, 1, keepdims=False)
        scale_col = lax.dynamic_index_in_dim(scales, column, 1, keepdims=False)
        taken = jnp.take(features, index_col, axis=1).astype(jnp.float32)
        return summed + taken * scale_col[None, :]

    summed = lax.fori_loop(0, fanout, add_slot, jnp.zeros((features.shape[0], dst_nodes), jnp.float32))
    return summed.astype(jnp.bfloat16)


def contract_rows(left, right_wide):
    return jnp.dot(jnp.transpose(left.astype(jnp.float32)), right_wide, preferred_element_type=jnp.float32)


def reference(features, weight_self, weight_neighbor, cotangent, source_tiles, neighbor_slots, neighbor_counts):
    mean_features = aggregate(features, source_tiles, neighbor_slots, neighbor_counts)
    own_features = features[:, :DST]
    wide_self = weight_self.astype(jnp.float32)
    wide_neighbor = weight_neighbor.astype(jnp.float32)
    preact = contract_rows(own_features, wide_self) + contract_rows(mean_features, wide_neighbor)
    activated = jax.nn.silu(preact).astype(jnp.bfloat16)
    sig_z = jax.nn.sigmoid(preact)
    grad_preact = (cotangent.astype(jnp.float32) * sig_z * (1.0 + preact * (1.0 - sig_z))).astype(jnp.bfloat16)
    wide_grad = grad_preact.astype(jnp.float32)
    grad_self = jnp.dot(own_features.astype(jnp.float32), wide_grad, preferred_element_type=jnp.float32)
    grad_neighbor = jnp.dot(mean_features.astype(jnp.float32), wide_grad, preferred_element_type=jnp.float32)
    return (activated, grad_self, grad_neighbor)
```

```python
import functools

import jax
import jax.numpy as jnp
from jax import lax
from jax.experimental import pallas as pl
from jax.experimental.pallas import tpu as pltpu
from jax.sharding import PartitionSpec as P

TILE = 128
SUB = 16
MESH = pl.DeviceIdType.MESH


def loop(lo, hi, body):
    def step(i, carry):
        body(i)
        return carry

    if hi > lo:
        lax.fori_loop(lo, hi, step, 0)


def grid_of(n):
    chips = n // 2
    rows = 1
    while rows * rows * 4 <= chips:
        rows *= 2
    return chips // rows, rows


def kernel(
    n,
    feat_ref,
    ws_hbm,
    wn_hbm,
    cot_ref,
    tiles_ref,
    slots_ref,
    counts_ref,
    act_ref,
    gs_ref,
    gn_ref,
    ws_ref,
    wn_ref,
    got_self,
    got_mean,
    mean_buf,
    feat_tiles,
    g_buf,
    grad_acc,
    w_sem,
    self_send,
    self_recv,
    mean_send,
    mean_recv,
    line_send,
    line_recv,
    row_send,
    row_recv,
    core_send,
    core_recv,
):
    me = lax.axis_index("feat")
    lines, rows = grid_of(n)
    core = lax.rem(me, 2)
    row = lax.rem(me // 2, rows)
    line = me // (2 * rows)
    width = feat_ref.shape[0]
    wire = got_self.dtype
    fanout = slots_ref.shape[0]
    listed = tiles_ref.shape[1]

    load_ws = pltpu.make_async_copy(ws_hbm, ws_ref, w_sem.at[0])
    load_wn = pltpu.make_async_copy(wn_hbm, wn_ref, w_sem.at[1])
    load_ws.start()
    load_wn.start()

    barrier = pltpu.get_barrier_semaphore()

    def greet(o):
        pl.semaphore_signal(
            barrier, inc=1, device_id={"feat": lax.rem(me + o, n)}, device_id_type=MESH
        )

    loop(1, n, greet)

    def columns(tile):
        return pl.ds(pl.multiple_of(tile * TILE, TILE), TILE)

    def split(t):
        feat_tiles[t] = feat_ref[:, columns(t)].astype(wire)

    for t in range(feat_ref.shape[1] // TILE):
        split(t)
    got_self[me] = feat_tiles[me]
    pl.semaphore_wait(barrier, n - 1)

    def self_copy(o):
        to = lax.rem(me + o, n)
        return pltpu.make_async_remote_copy(
            src_ref=feat_tiles.at[to],
            dst_ref=got_self.at[me],
            send_sem=self_send.at[o],
            recv_sem=self_recv.at[o],
            device_id={"feat": to},
            device_id_type=MESH,
        )

    def mean_copy(o):
        to = lax.rem(me + o, n)
        return pltpu.make_async_remote_copy(
            src_ref=mean_buf.at[to],
            dst_ref=got_mean.at[me],
            send_sem=mean_send.at[o],
            recv_sem=mean_recv.at[o],
            device_id={"feat": to},
            device_id_type=MESH,
        )

    loop(1, n, lambda o: self_copy(o).start())

    place = (
        lax.broadcasted_iota(jnp.int32, (TILE // SUB, SUB, TILE), 0) * SUB
        + lax.broadcasted_iota(jnp.int32, (TILE // SUB, SUB, TILE), 1)
    ).astype(jnp.int16)
    rank = lax.broadcasted_iota(jnp.int32, (fanout, TILE), 0)

    def mean_of(tile):
        slots = slots_ref[:, columns(tile)]
        counts = counts_ref[:, columns(tile)]
        slots = jnp.where(rank < counts, slots, -1)
        times = jnp.ones((fanout, TILE), jnp.float32)
        for j in range(fanout - 1):
            same = (slots == slots[j : j + 1, :]) & (rank > j)
            times += jnp.where(same, 1.0, 0.0)
        spot = [
            jnp.broadcast_to(slots[k : k + 1, :], (SUB, TILE)).astype(jnp.int16)[None]
            for k in range(fanout)
        ]
        often = [
            jnp.broadcast_to(times[k : k + 1, :], (SUB, TILE)).astype(jnp.bfloat16)[None]
            for k in range(fanout)
        ]
        summed = jnp.zeros((width, TILE), jnp.float32)
        for s in range(0, listed, 2):
            hot = []
            for h in range(2):
                here = place + jnp.int16((s + h) * TILE)
                part = jnp.zeros(here.shape, jnp.bfloat16)
                for k in range(fanout):
                    part = jnp.where(here == spot[k], often[k], part)
                hot.append(part.reshape(TILE, TILE))
            left = [feat_tiles[tiles_ref[tile, s + h]].astype(jnp.bfloat16) for h in range(2)]
            summed += jnp.dot(
                jnp.concatenate(left, axis=1),
                jnp.concatenate(hot, axis=0),
                preferred_element_type=jnp.float32,
            )
        scale = 1.0 / counts.astype(jnp.float32)
        return (summed * scale).astype(jnp.bfloat16).astype(wire)

    def aggregate(o):
        to = lax.rem(me + o, n)
        mean_buf[to] = mean_of(to)
        mean_copy(o).start()

    loop(1, n, aggregate)
    mine = mean_of(me)
    mean_buf[me] = mine
    got_mean[me] = mine

    def project(got, weight):
        x = got[...].reshape(n * width, TILE).astype(jnp.bfloat16)
        return lax.dot_general(
            x, weight[...], (((0,), (0,)), ((), ())), preferred_element_type=jnp.float32
        )

    load_ws.wait()
    loop(1, n, lambda o: self_copy(o).wait_recv())
    preact = project(got_self, ws_ref)
    load_wn.wait()
    loop(1, n, lambda o: mean_copy(o).wait_recv())
    preact += project(got_mean, wn_ref)

    sig = jax.nn.sigmoid(preact)
    cot = cot_ref[...].astype(jnp.float32)
    g_buf[me] = (cot * sig * (1.0 + preact * (1.0 - sig))).astype(jnp.bfloat16)

    def index(l, r, c):
        return (l * rows + r) * 2 + c

    def block(dl, dr, c):
        return index(lax.rem(line - dl + lines, lines), lax.rem(row - dr + rows, rows), c)

    def pass_on(slot, to, send, recv):
        return pltpu.make_async_remote_copy(
            src_ref=g_buf.at[slot],
            dst_ref=g_buf.at[slot],
            send_sem=send,
            recv_sem=recv,
            device_id={"feat": to},
            device_id_type=MESH,
        )

    def line_copy(dl, slot):
        to = index(lax.rem(line + dl, lines), row, core)
        return pass_on(slot, to, line_send.at[dl], line_recv.at[dl])

    def row_copy(dl, dr, slot):
        to = index(line, lax.rem(row + dr, rows), core)
        k = dl * rows + dr
        return pass_on(slot, to, row_send.at[k], row_recv.at[k])

    def core_copy(dl, dr, slot):
        k = dl * rows + dr
        return pass_on(slot, index(line, row, 1 - core), core_send.at[k], core_recv.at[k])

    loop(1, lines, lambda dl: line_copy(dl, me).start())
    loop(1, rows, lambda dr: row_copy(0, dr, me).start())
    core_copy(0, 0, me).start()
    act_ref[...] = (preact * sig).astype(jnp.bfloat16)
    grad_acc[...] = jnp.zeros_like(grad_acc)

    def add_block(slot):
        left = jnp.concatenate(
            [feat_tiles[slot].astype(jnp.bfloat16), mean_buf[slot].astype(jnp.bfloat16)], axis=0
        )
        grad_acc[...] += jnp.dot(left, g_buf[slot], preferred_element_type=jnp.float32)

    add_block(me)

    def from_line(dl):
        slot = block(dl, 0, core)
        line_copy(dl, slot).wait_recv()
        loop(1, rows, lambda dr: row_copy(dl, dr, slot).start())
        core_copy(dl, 0, slot).start()
        add_block(slot)

    loop(1, lines, from_line)

    def from_row(dl):
        def one(dr):
            slot = block(dl, dr, core)
            row_copy(dl, dr, slot).wait_recv()
            core_copy(dl, dr, slot).start()
            add_block(slot)

        loop(1, rows, one)

    loop(0, lines, from_row)

    def from_core(dl):
        def one(dr):
            slot = block(dl, dr, 1 - core)
            core_copy(dl, dr, slot).wait_recv()
            add_block(slot)

        loop(0, rows, one)

    loop(0, lines, from_core)
    gs_ref[...] = grad_acc[:width, :]
    gn_ref[...] = grad_acc[width:, :]

    loop(1, n, lambda o: self_copy(o).wait_send())
    loop(1, n, lambda o: mean_copy(o).wait_send())
    loop(1, lines, lambda dl: line_copy(dl, me).wait_send())

    def finish(dl):
        loop(1, rows, lambda dr: row_copy(dl, dr, block(dl, 0, core)).wait_send())
        loop(0, rows, lambda dr: core_copy(dl, dr, block(dl, dr, core)).wait_send())

    loop(0, lines, finish)


def on_device(
    n, features, weight_self, weight_neighbor, cotangent, source_tiles, neighbor_slots, neighbor_counts
):
    width = features.shape[0]
    hidden = weight_self.shape[1]
    dst_nodes = neighbor_counts.shape[0]
    assert dst_nodes == n * TILE and n % 2 == 0
    lines, rows = grid_of(n)
    wire = jnp.bfloat16 if width % SUB == 0 else jnp.float32
    vmem = pl.BlockSpec(memory_space=pltpu.VMEM)
    smem = pl.BlockSpec(memory_space=pltpu.SMEM)
    anywhere = pl.BlockSpec(memory_space=pl.ANY)
    slab = pltpu.VMEM((n, width, TILE), wire)
    dma = pltpu.SemaphoreType.DMA
    body = functools.partial(kernel, n)
    scratch = [
        pltpu.VMEM(weight_self.shape, jnp.bfloat16),
        pltpu.VMEM(weight_self.shape, jnp.bfloat16),
        slab,
        slab,
        slab,
        pltpu.VMEM((features.shape[1] // TILE, width, TILE), wire),
        pltpu.VMEM((n, TILE, hidden), jnp.bfloat16),
        pltpu.VMEM((2 * width, hidden), jnp.float32),
        dma((2,)),
        dma((n,)),
        dma((n,)),
        dma((n,)),
        dma((n,)),
        dma((lines,)),
        dma((lines,)),
        dma((lines * rows,)),
        dma((lines * rows,)),
        dma((lines * rows,)),
        dma((lines * rows,)),
    ]
    return pl.pallas_call(
        body,
        out_shape=(
            jax.ShapeDtypeStruct(cotangent.shape, jnp.bfloat16),
            jax.ShapeDtypeStruct((width, hidden), jnp.float32),
            jax.ShapeDtypeStruct((width, hidden), jnp.float32),
        ),
        in_specs=[vmem, anywhere, anywhere, vmem, smem, vmem, vmem],
        out_specs=(vmem, vmem, vmem),
        scratch_shapes=scratch,
        compiler_params=pltpu.CompilerParams(
            collective_id=0, has_side_effects=True, vmem_limit_bytes=32 * 1024 * 1024
        ),
        name="sage_layer",
    )(
        features,
        weight_self,
        weight_neighbor,
        cotangent,
        source_tiles,
        jnp.transpose(neighbor_slots),
        neighbor_counts.reshape(1, dst_nodes),
    )


def solution(mesh):
    in_specs = (
        P("feat", "groups"),
        P(),
        P(),
        P(("groups", "feat"), None),
        P("groups", None),
        P("groups", None),
        P("groups"),
    )
    out_specs = (
        P(("groups", "feat"), None),
        P(("groups", "feat"), None),
        P(("groups", "feat"), None),
    )
    return jax.shard_map(
        functools.partial(on_device, mesh.shape["feat"]),
        mesh=mesh,
        in_specs=in_specs,
        out_specs=out_specs,
        check_vma=False,
    )
```

```python
import functools

import jax
import jax.numpy as jnp
from jax import lax
from jax.experimental import pallas as pl
from jax.experimental.pallas import tpu as pltpu
from jax.sharding import PartitionSpec as P

TILE = 128
SUB = 16
MESH = pl.DeviceIdType.MESH


def loop(lo, hi, body):
    def step(i, carry):
        body(i)
        return carry

    if hi > lo:
        lax.fori_loop(lo, hi, step, 0)


def grid_of(n):
    chips = n // 2
    rows = 1
    while rows * rows * 4 <= chips:
        rows *= 2
    return chips // rows, rows


def kernel(
    n,
    feat_hbm,
    ws_hbm,
    wn_hbm,
    cot_hbm,
    tiles_hbm,
    slots_hbm,
    counts_hbm,
    act_ref,
    gs_ref,
    gn_ref,
    feat_ref,
    ws_ref,
    wn_ref,
    cot_ref,
    tiles_ref,
    slots_ref,
    counts_ref,
    got_self,
    got_mean,
    mean_buf,
    feat_tiles,
    g_buf,
    grad_acc,
    load_sem,
    self_send,
    self_recv,
    mean_send,
    mean_recv,
    line_send,
    line_recv,
    row_send,
    row_recv,
    core_send,
    core_recv,
):
    me = lax.axis_index("feat")
    lines, rows = grid_of(n)
    core = lax.rem(me, 2)
    row = lax.rem(me // 2, rows)
    line = me // (2 * rows)
    width = feat_ref.shape[0]
    wire = got_self.dtype
    fanout = slots_ref.shape[0]
    listed = tiles_ref.shape[1]

    loads = [
        pltpu.make_async_copy(src, dst, load_sem.at[i])
        for i, (src, dst) in enumerate(
            [
                (feat_hbm, feat_ref),
                (tiles_hbm, tiles_ref),
                (slots_hbm, slots_ref),
                (counts_hbm, counts_ref),
                (ws_hbm, ws_ref),
                (wn_hbm, wn_ref),
                (cot_hbm, cot_ref),
            ]
        )
    ]
    for load in loads:
        load.start()

    barrier = pltpu.get_barrier_semaphore()

    def greet(o):
        pl.semaphore_signal(
            barrier, inc=1, device_id={"feat": lax.rem(me + o, n)}, device_id_type=MESH
        )

    loop(1, n, greet)

    def columns(tile):
        return pl.ds(pl.multiple_of(tile * TILE, TILE), TILE)

    def split(t):
        feat_tiles[t] = feat_ref[:, columns(t)].astype(wire)

    loads[0].wait()
    for t in range(feat_ref.shape[1] // TILE):
        split(t)
    got_self[me] = feat_tiles[me]
    pl.semaphore_wait(barrier, n - 1)

    def self_copy(o):
        to = lax.rem(me + o, n)
        return pltpu.make_async_remote_copy(
            src_ref=feat_tiles.at[to],
            dst_ref=got_self.at[me],
            send_sem=self_send.at[o],
            recv_sem=self_recv.at[o],
            device_id={"feat": to},
            device_id_type=MESH,
        )

    def mean_copy(o):
        to = lax.rem(me + o, n)
        return pltpu.make_async_remote_copy(
            src_ref=mean_buf.at[to],
            dst_ref=got_mean.at[me],
            send_sem=mean_send.at[o],
            recv_sem=mean_recv.at[o],
            device_id={"feat": to},
            device_id_type=MESH,
        )

    loop(1, n, lambda o: self_copy(o).start())
    for load in loads[1:4]:
        load.wait()

    place = (
        lax.broadcasted_iota(jnp.int32, (TILE // SUB, SUB, TILE), 0) * SUB
        + lax.broadcasted_iota(jnp.int32, (TILE // SUB, SUB, TILE), 1)
    ).astype(jnp.int16)
    rank = lax.broadcasted_iota(jnp.int32, (fanout, TILE), 0)

    def mean_of(tile):
        slots = slots_ref[:, columns(tile)]
        counts = counts_ref[:, columns(tile)]
        slots = jnp.where(rank < counts, slots, -1)
        times = jnp.ones((fanout, TILE), jnp.float32)
        for j in range(fanout - 1):
            same = (slots == slots[j : j + 1, :]) & (rank > j)
            times += jnp.where(same, 1.0, 0.0)
        spot = [
            jnp.broadcast_to(slots[k : k + 1, :], (SUB, TILE)).astype(jnp.int16)[None]
            for k in range(fanout)
        ]
        often = [
            jnp.broadcast_to(times[k : k + 1, :], (SUB, TILE)).astype(jnp.bfloat16)[None]
            for k in range(fanout)
        ]
        summed = jnp.zeros((width, TILE), jnp.float32)
        for s in range(0, listed, 2):
            hot = []
            for h in range(2):
                here = place + jnp.int16((s + h) * TILE)
                part = jnp.zeros(here.shape, jnp.bfloat16)
                for k in range(fanout):
                    part = jnp.where(here == spot[k], often[k], part)
                hot.append(part.reshape(TILE, TILE))
            left = [feat_tiles[tiles_ref[tile, s + h]].astype(jnp.bfloat16) for h in range(2)]
            summed += jnp.dot(
                jnp.concatenate(left, axis=1),
                jnp.concatenate(hot, axis=0),
                preferred_element_type=jnp.float32,
            )
        scale = 1.0 / counts.astype(jnp.float32)
        return (summed * scale).astype(jnp.bfloat16).astype(wire)

    def aggregate(o):
        to = lax.rem(me + o, n)
        mean_buf[to] = mean_of(to)
        mean_copy(o).start()

    loop(1, n, aggregate)
    mine = mean_of(me)
    mean_buf[me] = mine
    got_mean[me] = mine

    def project(got, weight):
        x = got[...].reshape(n * width, TILE).astype(jnp.bfloat16)
        return lax.dot_general(
            x, weight[...], (((0,), (0,)), ((), ())), preferred_element_type=jnp.float32
        )

    for load in loads[4:]:
        load.wait()
    loop(1, n, lambda o: self_copy(o).wait_recv())
    preact = project(got_self, ws_ref)
    loop(1, n, lambda o: mean_copy(o).wait_recv())
    preact += project(got_mean, wn_ref)

    sig = jax.nn.sigmoid(preact)
    cot = cot_ref[...].astype(jnp.float32)
    g_buf[me] = (cot * sig * (1.0 + preact * (1.0 - sig))).astype(jnp.bfloat16)

    def index(l, r, c):
        return (l * rows + r) * 2 + c

    def block(dl, dr, c):
        return index(lax.rem(line - dl + lines, lines), lax.rem(row - dr + rows, rows), c)

    def pass_on(slot, to, send, recv):
        return pltpu.make_async_remote_copy(
            src_ref=g_buf.at[slot],
            dst_ref=g_buf.at[slot],
            send_sem=send,
            recv_sem=recv,
            device_id={"feat": to},
            device_id_type=MESH,
        )

    def line_copy(dl, slot):
        to = index(lax.rem(line + dl, lines), row, core)
        return pass_on(slot, to, line_send.at[dl], line_recv.at[dl])

    def row_copy(dl, dr, slot):
        to = index(line, lax.rem(row + dr, rows), core)
        k = dl * rows + dr
        return pass_on(slot, to, row_send.at[k], row_recv.at[k])

    def core_copy(dl, dr, slot):
        k = dl * rows + dr
        return pass_on(slot, index(line, row, 1 - core), core_send.at[k], core_recv.at[k])

    loop(1, lines, lambda dl: line_copy(dl, me).start())
    loop(1, rows, lambda dr: row_copy(0, dr, me).start())
    core_copy(0, 0, me).start()
    act_ref[...] = (preact * sig).astype(jnp.bfloat16)
    grad_acc[...] = jnp.zeros_like(grad_acc)

    def add_block(slot):
        left = jnp.concatenate(
            [feat_tiles[slot].astype(jnp.bfloat16), mean_buf[slot].astype(jnp.bfloat16)], axis=0
        )
        grad_acc[...] += jnp.dot(left, g_buf[slot], preferred_element_type=jnp.float32)

    add_block(me)

    def from_line(dl):
        slot = block(dl, 0, core)
        line_copy(dl, slot).wait_recv()
        loop(1, rows, lambda dr: row_copy(dl, dr, slot).start())
        core_copy(dl, 0, slot).start()
        add_block(slot)

    loop(1, lines, from_line)

    def from_row(dl):
        def one(dr):
            slot = block(dl, dr, core)
            row_copy(dl, dr, slot).wait_recv()
            core_copy(dl, dr, slot).start()
            add_block(slot)

        loop(1, rows, one)

    loop(0, lines, from_row)

    def from_core(dl):
        def one(dr):
            slot = block(dl, dr, 1 - core)
            core_copy(dl, dr, slot).wait_recv()
            add_block(slot)

        loop(0, rows, one)

    loop(0, lines, from_core)
    gs_ref[...] = grad_acc[:width, :]
    gn_ref[...] = grad_acc[width:, :]

    loop(1, n, lambda o: self_copy(o).wait_send())
    loop(1, n, lambda o: mean_copy(o).wait_send())
    loop(1, lines, lambda dl: line_copy(dl, me).wait_send())

    def finish(dl):
        loop(1, rows, lambda dr: row_copy(dl, dr, block(dl, 0, core)).wait_send())
        loop(0, rows, lambda dr: core_copy(dl, dr, block(dl, dr, core)).wait_send())

    loop(0, lines, finish)


def write_results(a_ref, b_ref, c_ref, a_out, b_out, c_out, sem):
    copies = [
        pltpu.make_async_copy(src, dst, sem.at[i])
        for i, (src, dst) in enumerate([(a_ref, a_out), (b_ref, b_out), (c_ref, c_out)])
    ]
    for copy in copies:
        copy.start()
    for copy in copies:
        copy.wait()


def on_device(
    n, features, weight_self, weight_neighbor, cotangent, source_tiles, neighbor_slots, neighbor_counts
):
    width = features.shape[0]
    hidden = weight_self.shape[1]
    dst_nodes = neighbor_counts.shape[0]
    assert dst_nodes == n * TILE and n % 2 == 0
    lines, rows = grid_of(n)
    wire = jnp.bfloat16 if width % SUB == 0 else jnp.float32
    vmem = pl.BlockSpec(memory_space=pltpu.VMEM)
    hbm = pl.BlockSpec(memory_space=pltpu.HBM)
    slab = pltpu.VMEM((n, width, TILE), wire)
    dma = pltpu.SemaphoreType.DMA
    body = functools.partial(kernel, n)
    scratch = [
        pltpu.VMEM(features.shape, jnp.bfloat16),
        pltpu.VMEM(weight_self.shape, jnp.bfloat16),
        pltpu.VMEM(weight_self.shape, jnp.bfloat16),
        pltpu.VMEM(cotangent.shape, jnp.bfloat16),
        pltpu.SMEM(source_tiles.shape, jnp.int32),
        pltpu.VMEM(neighbor_slots.shape[::-1], jnp.int32),
        pltpu.VMEM((1, dst_nodes), jnp.int32),
        slab,
        slab,
        slab,
        pltpu.VMEM((features.shape[1] // TILE, width, TILE), wire),
        pltpu.VMEM((n, TILE, hidden), jnp.bfloat16),
        pltpu.VMEM((2 * width, hidden), jnp.float32),
        dma((7,)),
        dma((n,)),
        dma((n,)),
        dma((n,)),
        dma((n,)),
        dma((lines,)),
        dma((lines,)),
        dma((lines * rows,)),
        dma((lines * rows,)),
        dma((lines * rows,)),
        dma((lines * rows,)),
    ]
    held = pl.pallas_call(
        body,
        out_shape=(
            jax.ShapeDtypeStruct(cotangent.shape, jnp.bfloat16),
            jax.ShapeDtypeStruct((width, hidden), jnp.float32),
            jax.ShapeDtypeStruct((width, hidden), jnp.float32),
        ),
        in_specs=[hbm] * 7,
        out_specs=(vmem, vmem, vmem),
        scratch_shapes=scratch,
        compiler_params=pltpu.CompilerParams(
            collective_id=0, has_side_effects=True, vmem_limit_bytes=64 * 1024 * 1024
        ),
        name="sage_layer",
    )(
        features,
        weight_self,
        weight_neighbor,
        cotangent,
        source_tiles,
        jnp.transpose(neighbor_slots),
        neighbor_counts.reshape(1, dst_nodes),
    )
    return pl.pallas_call(
        write_results,
        out_shape=tuple(jax.ShapeDtypeStruct(x.shape, x.dtype) for x in held),
        in_specs=[vmem] * 3,
        out_specs=(hbm, hbm, hbm),
        scratch_shapes=[dma((3,))],
        name="write_results",
    )(*held)


def solution(mesh):
    in_specs = (
        P("feat", "groups"),
        P(),
        P(),
        P(("groups", "feat"), None),
        P("groups", None),
        P("groups", None),
        P("groups"),
    )
    out_specs = (
        P(("groups", "feat"), None),
        P(("groups", "feat"), None),
        P(("groups", "feat"), None),
    )
    return jax.shard_map(
        functools.partial(on_device, mesh.shape["feat"]),
        mesh=mesh,
        in_specs=in_specs,
        out_specs=out_specs,
        check_vma=False,
    )
```

```python
import functools

import jax
import jax.numpy as jnp
from jax import lax
from jax.experimental import pallas as pl
from jax.experimental.pallas import tpu as pltpu
from jax.sharding import PartitionSpec as P

TILE = 128
SUB = 16
UNROLL = 16
MESH = pl.DeviceIdType.MESH


def loop(lo, hi, body):
    def step(i, carry):
        body(i)
        return carry

    if hi - lo <= UNROLL:
        for i in range(lo, hi):
            body(i)
    else:
        lax.fori_loop(lo, hi, step, 0)


def wrap(i, n):
    return jnp.where(i >= n, i - n, i)


def grid_of(n):
    chips = n // 2
    rows = 1
    while rows * rows * 4 <= chips:
        rows *= 2
    return chips // rows, rows


def kernel(
    n,
    feat_hbm,
    ws_hbm,
    wn_hbm,
    cot_hbm,
    tiles_hbm,
    slots_hbm,
    counts_hbm,
    act_ref,
    gs_ref,
    gn_ref,
    feat_ref,
    ws_ref,
    wn_ref,
    cot_ref,
    tiles_ref,
    slots_ref,
    counts_ref,
    got_self,
    got_mean,
    mean_buf,
    feat_tiles,
    g_buf,
    grad_acc,
    load_sem,
    self_send,
    self_recv,
    mean_send,
    mean_recv,
    line_send,
    line_recv,
    row_send,
    row_recv,
    core_send,
    core_recv,
):
    me = lax.axis_index("feat")
    lines, rows = grid_of(n)
    core = lax.rem(me, 2)
    row = lax.rem(me // 2, rows)
    line = me // (2 * rows)
    width = feat_ref.shape[0]
    wire = got_self.dtype
    fanout = slots_ref.shape[0]
    listed = tiles_ref.shape[1]

    loads = [
        pltpu.make_async_copy(src, dst, load_sem.at[i])
        for i, (src, dst) in enumerate(
            [
                (feat_hbm, feat_ref),
                (tiles_hbm, tiles_ref),
                (slots_hbm, slots_ref),
                (counts_hbm, counts_ref),
                (ws_hbm, ws_ref),
                (wn_hbm, wn_ref),
                (cot_hbm, cot_ref),
            ]
        )
    ]
    for load in loads:
        load.start()

    barrier = pltpu.get_barrier_semaphore()

    def greet(o):
        pl.semaphore_signal(
            barrier, inc=1, device_id={"feat": wrap(me + o, n)}, device_id_type=MESH
        )

    loop(1, n, greet)

    def columns(tile):
        return pl.ds(pl.multiple_of(tile * TILE, TILE), TILE)

    def split(t):
        feat_tiles[t] = feat_ref[:, columns(t)].astype(wire)

    loads[0].wait()
    for t in range(feat_ref.shape[1] // TILE):
        split(t)
    got_self[me] = feat_tiles[me]
    pl.semaphore_wait(barrier, n - 1)

    def self_copy(o):
        to = wrap(me + o, n)
        return pltpu.make_async_remote_copy(
            src_ref=feat_tiles.at[to],
            dst_ref=got_self.at[me],
            send_sem=self_send.at[o],
            recv_sem=self_recv.at[o],
            device_id={"feat": to},
            device_id_type=MESH,
        )

    def mean_copy(o):
        to = wrap(me + o, n)
        return pltpu.make_async_remote_copy(
            src_ref=mean_buf.at[to],
            dst_ref=got_mean.at[me],
            send_sem=mean_send.at[o],
            recv_sem=mean_recv.at[o],
            device_id={"feat": to},
            device_id_type=MESH,
        )

    loop(1, n, lambda o: self_copy(o).start())
    for load in loads[1:4]:
        load.wait()

    place = (
        lax.broadcasted_iota(jnp.int32, (TILE // SUB, SUB, TILE), 0) * SUB
        + lax.broadcasted_iota(jnp.int32, (TILE // SUB, SUB, TILE), 1)
    ).astype(jnp.int16)
    rank = lax.broadcasted_iota(jnp.int32, (fanout, TILE), 0)

    def mean_of(tile):
        slots = slots_ref[:, columns(tile)]
        counts = counts_ref[:, columns(tile)]
        slots = jnp.where(rank < counts, slots, -1)
        times = jnp.ones((fanout, TILE), jnp.float32)
        for j in range(fanout - 1):
            same = (slots == slots[j : j + 1, :]) & (rank > j)
            times += jnp.where(same, 1.0, 0.0)
        spot = [
            jnp.broadcast_to(slots[k : k + 1, :], (SUB, TILE)).astype(jnp.int16)[None]
            for k in range(fanout)
        ]
        often = [
            jnp.broadcast_to(times[k : k + 1, :], (SUB, TILE)).astype(jnp.bfloat16)[None]
            for k in range(fanout)
        ]
        summed = jnp.zeros((width, TILE), jnp.float32)
        for s in range(0, listed, 2):
            hot = []
            for h in range(2):
                here = place + jnp.int16((s + h) * TILE)
                part = jnp.zeros(here.shape, jnp.bfloat16)
                for k in range(fanout):
                    part = jnp.where(here == spot[k], often[k], part)
                hot.append(part.reshape(TILE, TILE))
            left = [feat_tiles[tiles_ref[tile, s + h]].astype(jnp.bfloat16) for h in range(2)]
            summed += jnp.dot(
                jnp.concatenate(left, axis=1),
                jnp.concatenate(hot, axis=0),
                preferred_element_type=jnp.float32,
            )
        scale = 1.0 / counts.astype(jnp.float32)
        return (summed * scale).astype(jnp.bfloat16).astype(wire)

    def aggregate(o):
        to = wrap(me + o, n)
        mean_buf[to] = mean_of(to)
        mean_copy(o).start()

    lax.fori_loop(1, n, lambda o, carry: (aggregate(o), carry)[1], 0)
    mine = mean_of(me)
    mean_buf[me] = mine
    got_mean[me] = mine

    def project(got, weight):
        x = got[...].reshape(n * width, TILE).astype(jnp.bfloat16)
        return lax.dot_general(
            x, weight[...], (((0,), (0,)), ((), ())), preferred_element_type=jnp.float32
        )

    for load in loads[4:]:
        load.wait()
    loop(1, n, lambda o: self_copy(o).wait_recv())
    preact = project(got_self, ws_ref)
    loop(1, n, lambda o: mean_copy(o).wait_recv())
    preact += project(got_mean, wn_ref)

    sig = jax.nn.sigmoid(preact)
    cot = cot_ref[...].astype(jnp.float32)
    g_buf[me] = (cot * sig * (1.0 + preact * (1.0 - sig))).astype(jnp.bfloat16)

    def index(l, r, c):
        return (l * rows + r) * 2 + c

    def block(dl, dr, c):
        return index(wrap(line - dl + lines, lines), wrap(row - dr + rows, rows), c)

    def pass_on(slot, to, send, recv):
        return pltpu.make_async_remote_copy(
            src_ref=g_buf.at[slot],
            dst_ref=g_buf.at[slot],
            send_sem=send,
            recv_sem=recv,
            device_id={"feat": to},
            device_id_type=MESH,
        )

    def line_copy(dl, slot):
        to = index(wrap(line + dl, lines), row, core)
        return pass_on(slot, to, line_send.at[dl], line_recv.at[dl])

    def row_copy(dl, dr, slot):
        to = index(line, wrap(row + dr, rows), core)
        k = dl * rows + dr
        return pass_on(slot, to, row_send.at[k], row_recv.at[k])

    def core_copy(dl, dr, slot):
        k = dl * rows + dr
        return pass_on(slot, index(line, row, 1 - core), core_send.at[k], core_recv.at[k])

    loop(1, lines, lambda dl: line_copy(dl, me).start())
    loop(1, rows, lambda dr: row_copy(0, dr, me).start())
    core_copy(0, 0, me).start()
    act_ref[...] = (preact * sig).astype(jnp.bfloat16)
    grad_acc[...] = jnp.zeros_like(grad_acc)

    def add_block(slot):
        left = jnp.concatenate(
            [feat_tiles[slot].astype(jnp.bfloat16), mean_buf[slot].astype(jnp.bfloat16)], axis=0
        )
        grad_acc[...] += jnp.dot(left, g_buf[slot], preferred_element_type=jnp.float32)

    add_block(me)

    def from_line(dl):
        slot = block(dl, 0, core)
        line_copy(dl, slot).wait_recv()
        loop(1, rows, lambda dr: row_copy(dl, dr, slot).start())
        core_copy(dl, 0, slot).start()
        add_block(slot)

    loop(1, lines, from_line)

    def from_row(dl):
        def one(dr):
            slot = block(dl, dr, core)
            row_copy(dl, dr, slot).wait_recv()
            core_copy(dl, dr, slot).start()
            add_block(slot)

        loop(1, rows, one)

    loop(0, lines, from_row)

    def from_core(dl):
        def one(dr):
            slot = block(dl, dr, 1 - core)
            core_copy(dl, dr, slot).wait_recv()
            add_block(slot)

        loop(0, rows, one)

    loop(0, lines, from_core)
    gs_ref[...] = grad_acc[:width, :]
    gn_ref[...] = grad_acc[width:, :]

    loop(1, n, lambda o: self_copy(o).wait_send())
    loop(1, n, lambda o: mean_copy(o).wait_send())
    loop(1, lines, lambda dl: line_copy(dl, me).wait_send())

    def finish(dl):
        loop(1, rows, lambda dr: row_copy(dl, dr, block(dl, 0, core)).wait_send())
        loop(0, rows, lambda dr: core_copy(dl, dr, block(dl, dr, core)).wait_send())

    loop(0, lines, finish)


def write_results(a_ref, b_ref, c_ref, a_out, b_out, c_out, sem):
    copies = [
        pltpu.make_async_copy(src, dst, sem.at[i])
        for i, (src, dst) in enumerate([(a_ref, a_out), (b_ref, b_out), (c_ref, c_out)])
    ]
    for copy in copies:
        copy.start()
    for copy in copies:
        copy.wait()


def on_device(
    n, features, weight_self, weight_neighbor, cotangent, source_tiles, neighbor_slots, neighbor_counts
):
    width = features.shape[0]
    hidden = weight_self.shape[1]
    dst_nodes = neighbor_counts.shape[0]
    assert dst_nodes == n * TILE and n % 2 == 0
    lines, rows = grid_of(n)
    wire = jnp.bfloat16 if width % SUB == 0 else jnp.float32
    vmem = pl.BlockSpec(memory_space=pltpu.VMEM)
    hbm = pl.BlockSpec(memory_space=pltpu.HBM)
    slab = pltpu.VMEM((n, width, TILE), wire)
    dma = pltpu.SemaphoreType.DMA
    body = functools.partial(kernel, n)
    scratch = [
        pltpu.VMEM(features.shape, jnp.bfloat16),
        pltpu.VMEM(weight_self.shape, jnp.bfloat16),
        pltpu.VMEM(weight_self.shape, jnp.bfloat16),
        pltpu.VMEM(cotangent.shape, jnp.bfloat16),
        pltpu.SMEM(source_tiles.shape, jnp.int32),
        pltpu.VMEM(neighbor_slots.shape[::-1], jnp.int32),
        pltpu.VMEM((1, dst_nodes), jnp.int32),
        slab,
        slab,
        slab,
        pltpu.VMEM((features.shape[1] // TILE, width, TILE), wire),
        pltpu.VMEM((n, TILE, hidden), jnp.bfloat16),
        pltpu.VMEM((2 * width, hidden), jnp.float32),
        dma((7,)),
        dma((n,)),
        dma((n,)),
        dma((n,)),
        dma((n,)),
        dma((lines,)),
        dma((lines,)),
        dma((lines * rows,)),
        dma((lines * rows,)),
        dma((lines * rows,)),
        dma((lines * rows,)),
    ]
    held = pl.pallas_call(
        body,
        out_shape=(
            jax.ShapeDtypeStruct(cotangent.shape, jnp.bfloat16),
            jax.ShapeDtypeStruct((width, hidden), jnp.float32),
            jax.ShapeDtypeStruct((width, hidden), jnp.float32),
        ),
        in_specs=[hbm] * 7,
        out_specs=(vmem, vmem, vmem),
        scratch_shapes=scratch,
        compiler_params=pltpu.CompilerParams(
            collective_id=0, has_side_effects=True, vmem_limit_bytes=64 * 1024 * 1024
        ),
        name="sage_layer",
    )(
        features,
        weight_self,
        weight_neighbor,
        cotangent,
        source_tiles,
        jnp.transpose(neighbor_slots),
        neighbor_counts.reshape(1, dst_nodes),
    )
    return pl.pallas_call(
        write_results,
        out_shape=tuple(jax.ShapeDtypeStruct(x.shape, x.dtype) for x in held),
        in_specs=[vmem] * 3,
        out_specs=(hbm, hbm, hbm),
        scratch_shapes=[dma((3,))],
        name="write_results",
    )(*held)


def solution(mesh):
    in_specs = (
        P("feat", "groups"),
        P(),
        P(),
        P(("groups", "feat"), None),
        P("groups", None),
        P("groups", None),
        P("groups"),
    )
    out_specs = (
        P(("groups", "feat"), None),
        P(("groups", "feat"), None),
        P(("groups", "feat"), None),
    )
    return jax.shard_map(
        functools.partial(on_device, mesh.shape["feat"]),
        mesh=mesh,
        in_specs=in_specs,
        out_specs=out_specs,
        check_vma=False,
    )
```

```python
import functools

import jax
import jax.numpy as jnp
from jax import lax
from jax.experimental import pallas as pl
from jax.experimental.pallas import tpu as pltpu
from jax.sharding import PartitionSpec as P

TILE = 128
SUB = 16
UNROLL = 16
MESH = pl.DeviceIdType.MESH


def loop(lo, hi, body):
    def step(i, carry):
        body(i)
        return carry

    if hi - lo <= UNROLL:
        for i in range(lo, hi):
            body(i)
    else:
        lax.fori_loop(lo, hi, step, 0)


def wrap(i, n):
    return jnp.where(i >= n, i - n, i)


def grid_of(n):
    chips = n // 2
    rows = 1
    while rows * rows * 4 <= chips:
        rows *= 2
    return chips // rows, rows


def kernel(
    n,
    feat_hbm,
    ws_hbm,
    wn_hbm,
    cot_hbm,
    tiles_hbm,
    slots_hbm,
    counts_hbm,
    act_ref,
    gs_ref,
    gn_ref,
    feat_ref,
    ws_ref,
    wn_ref,
    cot_ref,
    tiles_ref,
    slots_ref,
    counts_ref,
    got_self,
    got_mean,
    mean_buf,
    feat_tiles,
    g_buf,
    grad_acc,
    load_sem,
    self_send,
    self_recv,
    mean_send,
    mean_recv,
    line_send,
    line_recv,
    row_send,
    row_recv,
    core_send,
    core_recv,
):
    me = lax.axis_index("feat")
    lines, rows = grid_of(n)
    core = lax.rem(me, 2)
    row = lax.rem(me // 2, rows)
    line = me // (2 * rows)
    width = feat_ref.shape[0]
    wire = got_self.dtype
    fanout = slots_ref.shape[0]
    listed = tiles_ref.shape[1]

    loads = [
        pltpu.make_async_copy(src, dst, load_sem.at[i])
        for i, (src, dst) in enumerate(
            [
                (feat_hbm, feat_ref),
                (tiles_hbm, tiles_ref),
                (slots_hbm, slots_ref),
                (counts_hbm, counts_ref),
                (ws_hbm, ws_ref),
                (wn_hbm, wn_ref),
                (cot_hbm, cot_ref),
            ]
        )
    ]
    for load in loads:
        load.start()

    barrier = pltpu.get_barrier_semaphore()

    def greet(o):
        pl.semaphore_signal(
            barrier, inc=1, device_id={"feat": wrap(me + o, n)}, device_id_type=MESH
        )

    loop(1, n, greet)

    def columns(tile):
        return pl.ds(pl.multiple_of(tile * TILE, TILE), TILE)

    def split(t):
        feat_tiles[t] = feat_ref[:, columns(t)].astype(wire)

    loads[0].wait()
    straight = feat_ref.dtype == wire

    def cut():
        for t in range(feat_ref.shape[1] // TILE):
            split(t)
        got_self[me] = feat_tiles[me]

    if not straight:
        cut()
    pl.semaphore_wait(barrier, n - 1)

    def self_copy(o):
        to = wrap(me + o, n)
        return pltpu.make_async_remote_copy(
            src_ref=feat_ref.at[:, columns(to)] if straight else feat_tiles.at[to],
            dst_ref=got_self.at[me],
            send_sem=self_send.at[o],
            recv_sem=self_recv.at[o],
            device_id={"feat": to},
            device_id_type=MESH,
        )

    def mean_copy(o):
        to = wrap(me + o, n)
        return pltpu.make_async_remote_copy(
            src_ref=mean_buf.at[to],
            dst_ref=got_mean.at[me],
            send_sem=mean_send.at[o],
            recv_sem=mean_recv.at[o],
            device_id={"feat": to},
            device_id_type=MESH,
        )

    loop(1, n, lambda o: self_copy(o).start())
    if straight:
        cut()
    for load in loads[1:4]:
        load.wait()

    place = (
        lax.broadcasted_iota(jnp.int32, (TILE // SUB, SUB, TILE), 0) * SUB
        + lax.broadcasted_iota(jnp.int32, (TILE // SUB, SUB, TILE), 1)
    ).astype(jnp.int16)
    rank = lax.broadcasted_iota(jnp.int32, (fanout, TILE), 0)

    def mean_of(tile):
        slots = slots_ref[:, columns(tile)]
        counts = counts_ref[:, columns(tile)]
        slots = jnp.where(rank < counts, slots, -1)
        times = jnp.ones((fanout, TILE), jnp.float32)
        for j in range(fanout - 1):
            same = (slots == slots[j : j + 1, :]) & (rank > j)
            times += jnp.where(same, 1.0, 0.0)
        spot = [
            jnp.broadcast_to(slots[k : k + 1, :], (SUB, TILE)).astype(jnp.int16)[None]
            for k in range(fanout)
        ]
        often = [
            jnp.broadcast_to(times[k : k + 1, :], (SUB, TILE)).astype(jnp.bfloat16)[None]
            for k in range(fanout)
        ]
        summed = jnp.zeros((width, TILE), jnp.float32)
        for s in range(0, listed, 2):
            hot = []
            for h in range(2):
                here = place + jnp.int16((s + h) * TILE)
                part = jnp.zeros(here.shape, jnp.bfloat16)
                for k in range(fanout):
                    part = jnp.where(here == spot[k], often[k], part)
                hot.append(part.reshape(TILE, TILE))
            left = [feat_tiles[tiles_ref[tile, s + h]].astype(jnp.bfloat16) for h in range(2)]
            summed += jnp.dot(
                jnp.concatenate(left, axis=1),
                jnp.concatenate(hot, axis=0),
                preferred_element_type=jnp.float32,
            )
        scale = 1.0 / counts.astype(jnp.float32)
        return (summed * scale).astype(jnp.bfloat16).astype(wire)

    def aggregate(o):
        to = wrap(me + o, n)
        mean_buf[to] = mean_of(to)
        mean_copy(o).start()

    lax.fori_loop(1, n, lambda o, carry: (aggregate(o), carry)[1], 0)
    mine = mean_of(me)
    mean_buf[me] = mine
    got_mean[me] = mine

    def project(got, weight):
        x = got[...].reshape(n * width, TILE).astype(jnp.bfloat16)
        return lax.dot_general(
            x, weight[...], (((0,), (0,)), ((), ())), preferred_element_type=jnp.float32
        )

    for load in loads[4:]:
        load.wait()
    loop(1, n, lambda o: self_copy(o).wait_recv())
    preact = project(got_self, ws_ref)
    loop(1, n, lambda o: mean_copy(o).wait_recv())
    preact += project(got_mean, wn_ref)

    sig = jax.nn.sigmoid(preact)
    cot = cot_ref[...].astype(jnp.float32)
    g_buf[me] = (cot * sig * (1.0 + preact * (1.0 - sig))).astype(jnp.bfloat16)

    def index(l, r, c):
        return (l * rows + r) * 2 + c

    def block(dl, dr, c):
        return index(wrap(line - dl + lines, lines), wrap(row - dr + rows, rows), c)

    def pass_on(slot, to, send, recv):
        return pltpu.make_async_remote_copy(
            src_ref=g_buf.at[slot],
            dst_ref=g_buf.at[slot],
            send_sem=send,
            recv_sem=recv,
            device_id={"feat": to},
            device_id_type=MESH,
        )

    def line_copy(dl, slot):
        to = index(wrap(line + dl, lines), row, core)
        return pass_on(slot, to, line_send.at[dl], line_recv.at[dl])

    def row_copy(dl, dr, slot):
        to = index(line, wrap(row + dr, rows), core)
        k = dl * rows + dr
        return pass_on(slot, to, row_send.at[k], row_recv.at[k])

    def core_copy(dl, dr, slot):
        k = dl * rows + dr
        return pass_on(slot, index(line, row, 1 - core), core_send.at[k], core_recv.at[k])

    loop(1, lines, lambda dl: line_copy(dl, me).start())
    loop(1, rows, lambda dr: row_copy(0, dr, me).start())
    core_copy(0, 0, me).start()
    act_ref[...] = (preact * sig).astype(jnp.bfloat16)
    grad_acc[...] = jnp.zeros_like(grad_acc)

    def add_block(slot):
        left = jnp.concatenate(
            [feat_tiles[slot].astype(jnp.bfloat16), mean_buf[slot].astype(jnp.bfloat16)], axis=0
        )
        grad_acc[...] += jnp.dot(left, g_buf[slot], preferred_element_type=jnp.float32)

    add_block(me)

    def from_line(dl):
        slot = block(dl, 0, core)
        line_copy(dl, slot).wait_recv()
        loop(1, rows, lambda dr: row_copy(dl, dr, slot).start())
        core_copy(dl, 0, slot).start()
        add_block(slot)

    loop(1, lines, from_line)

    def from_row(dl):
        def one(dr):
            slot = block(dl, dr, core)
            row_copy(dl, dr, slot).wait_recv()
            core_copy(dl, dr, slot).start()
            add_block(slot)

        loop(1, rows, one)

    loop(0, lines, from_row)

    def from_core(dl):
        def one(dr):
            slot = block(dl, dr, 1 - core)
            core_copy(dl, dr, slot).wait_recv()
            add_block(slot)

        loop(0, rows, one)

    loop(0, lines, from_core)
    gs_ref[...] = grad_acc[:width, :]
    gn_ref[...] = grad_acc[width:, :]

    loop(1, n, lambda o: self_copy(o).wait_send())
    loop(1, n, lambda o: mean_copy(o).wait_send())
    loop(1, lines, lambda dl: line_copy(dl, me).wait_send())

    def finish(dl):
        loop(1, rows, lambda dr: row_copy(dl, dr, block(dl, 0, core)).wait_send())
        loop(0, rows, lambda dr: core_copy(dl, dr, block(dl, dr, core)).wait_send())

    loop(0, lines, finish)


def write_results(a_ref, b_ref, c_ref, a_out, b_out, c_out, sem):
    copies = [
        pltpu.make_async_copy(src, dst, sem.at[i])
        for i, (src, dst) in enumerate([(a_ref, a_out), (b_ref, b_out), (c_ref, c_out)])
    ]
    for copy in copies:
        copy.start()
    for copy in copies:
        copy.wait()


def on_device(
    n, features, weight_self, weight_neighbor, cotangent, source_tiles, neighbor_slots, neighbor_counts
):
    width = features.shape[0]
    hidden = weight_self.shape[1]
    dst_nodes = neighbor_counts.shape[0]
    assert dst_nodes == n * TILE and n % 2 == 0
    lines, rows = grid_of(n)
    wire = jnp.bfloat16 if width % SUB == 0 else jnp.float32
    vmem = pl.BlockSpec(memory_space=pltpu.VMEM)
    hbm = pl.BlockSpec(memory_space=pltpu.HBM)
    slab = pltpu.VMEM((n, width, TILE), wire)
    dma = pltpu.SemaphoreType.DMA
    body = functools.partial(kernel, n)
    scratch = [
        pltpu.VMEM(features.shape, jnp.bfloat16),
        pltpu.VMEM(weight_self.shape, jnp.bfloat16),
        pltpu.VMEM(weight_self.shape, jnp.bfloat16),
        pltpu.VMEM(cotangent.shape, jnp.bfloat16),
        pltpu.SMEM(source_tiles.shape, jnp.int32),
        pltpu.VMEM(neighbor_slots.shape[::-1], jnp.int32),
        pltpu.VMEM((1, dst_nodes), jnp.int32),
        slab,
        slab,
        slab,
        pltpu.VMEM((features.shape[1] // TILE, width, TILE), wire),
        pltpu.VMEM((n, TILE, hidden), jnp.bfloat16),
        pltpu.VMEM((2 * width, hidden), jnp.float32),
        dma((7,)),
        dma((n,)),
        dma((n,)),
        dma((n,)),
        dma((n,)),
        dma((lines,)),
        dma((lines,)),
        dma((lines * rows,)),
        dma((lines * rows,)),
        dma((lines * rows,)),
        dma((lines * rows,)),
    ]
    held = pl.pallas_call(
        body,
        out_shape=(
            jax.ShapeDtypeStruct(cotangent.shape, jnp.bfloat16),
            jax.ShapeDtypeStruct((width, hidden), jnp.float32),
            jax.ShapeDtypeStruct((width, hidden), jnp.float32),
        ),
        in_specs=[hbm] * 7,
        out_specs=(vmem, vmem, vmem),
        scratch_shapes=scratch,
        compiler_params=pltpu.CompilerParams(
            collective_id=0, has_side_effects=True, vmem_limit_bytes=64 * 1024 * 1024
        ),
        name="sage_layer",
    )(
        features,
        weight_self,
        weight_neighbor,
        cotangent,
        source_tiles,
        jnp.transpose(neighbor_slots),
        neighbor_counts.reshape(1, dst_nodes),
    )
    return pl.pallas_call(
        write_results,
        out_shape=tuple(jax.ShapeDtypeStruct(x.shape, x.dtype) for x in held),
        in_specs=[vmem] * 3,
        out_specs=(hbm, hbm, hbm),
        scratch_shapes=[dma((3,))],
        name="write_results",
    )(*held)


def solution(mesh):
    in_specs = (
        P("feat", "groups"),
        P(),
        P(),
        P(("groups", "feat"), None),
        P("groups", None),
        P("groups", None),
        P("groups"),
    )
    out_specs = (
        P(("groups", "feat"), None),
        P(("groups", "feat"), None),
        P(("groups", "feat"), None),
    )
    return jax.shard_map(
        functools.partial(on_device, mesh.shape["feat"]),
        mesh=mesh,
        in_specs=in_specs,
        out_specs=out_specs,
        check_vma=False,
    )
```
